32 devices in a mesh: section: 4 (over z), tensor: 8 (over y, x, core).
Axes of the slice: x: 2, y: 2, z: 4, core: 2. Of those that a mesh axis runs over, the one named last changes fastest.
Arguments:
- acts_prev: bfloat16 [2048, 8192], P('section', 'tensor'), may hold values from -6 to 6
- embedded: bfloat16 [512, 8192], P(None, 'tensor'), may hold values from -6 to 6
- grads_next: bfloat16 [2048, 8192], P('section', 'tensor'), may hold values from -1.5 to 1.5
- loss_grad: bfloat16 [512, 8192], P(None, 'tensor'), may hold values from -1.5 to 1.5
- up_weight: bfloat16 [4, 2, 256, 32768], P('section', None, None, 'tensor'), may hold values from -0.25 to 0.25
- down_weight: bfloat16 [4, 2, 32768, 256], P('section', None, 'tensor'), may hold values from -0.125 to 0.125
Outputs:
- mixed: bfloat16 [2048, 8192], P('section', 'tensor')
- input_grads: bfloat16 [2048, 8192], P('section', 'tensor')
- up_grad: bfloat16 [4, 2, 256, 32768], P('section', None, None, 'tensor')
- down_grad: bfloat16 [4, 2, 32768, 256], P('section', None, 'tensor')
The draws below stay inside these ranges and needn't reach their ends.
All inputs are finite; a program needn't handle non-finite values.
Results may differ from the reference program's by a relative error of at most 0.005.
Values may be sent and summed in bfloat16 or wider, within the bound.
No kernel may reach another device: no remote copies, remote signals or barrier semaphores. Data moves between devices by JAX's collectives and lax.ppermute only.
A program may use at most 64 MiB of HBM per device.

```python
import jax
import jax.numpy as jnp
from jax import lax

D = 8192
H = 32768
BLK = 256
LEVELS = 1
TOK = 512
DBLOCKS = 32
HBLOCKS = 128
EXPAND = 4
N_SECTION = 4
N_TENSOR = 8


def shard_levels(own_key, shape, pieces, least, largest):
    loudness = 1.0
    for axis_at, parts in pieces:
        heights = jax.random.uniform(jax.random.fold_in(jax.random.fold_in(own_key, 6), axis_at), (parts,), jnp.float32, least / len(pieces), largest / len(pieces))
        loudness = loudness * jnp.repeat(jnp.exp(heights), shape[axis_at] // parts).reshape((-1,) + (1,) * (len(shape) - 1 - axis_at))
    return loudness


def centred(stream_key, dims, scale, limit, pieces=(), kind=jnp.bfloat16):
    drawn = scale * jax.random.normal(stream_key, dims, jnp.float32)
    if pieces:
        drawn = drawn * shard_levels(stream_key, dims, pieces, -0.22, 0.18)
    return jnp.clip(drawn, -limit, limit).astype(kind)


def setup_inputs(seed: int = 0) -> dict:
    streams_of = jax.random.split(jax.random.key(seed), 7)
    acts_prev = centred(streams_of[0], (N_SECTION * TOK, D), 1.0, 6.0, ((0, 4), (1, 8)))
    embedded = centred(streams_of[1], (TOK, D), 1.0, 6.0, ((1, 8),))
    grads_next = centred(streams_of[2], (N_SECTION * TOK, D), 0.25, 1.5, ((0, 4), (1, 8)))
    loss_grad = centred(streams_of[3], (TOK, D), 0.25, 1.5, ((1, 8),))
    up_weight = centred(streams_of[4], (N_SECTION, LEVELS + 1, BLK, H), ((LEVELS + 1) * BLK) ** -0.5, 0.25, ((0, 4), (3, 8)))
    down_weight = centred(streams_of[5], (N_SECTION, LEVELS + 1, H, BLK), ((LEVELS + 1) * EXPAND * BLK) ** -0.5, 0.125, ((0, 4), (2, 8)))
    return {"acts_prev": acts_prev, "embedded": embedded, "grads_next": grads_next, "loss_grad": loss_grad, "up_weight": up_weight, "down_weight": down_weight}


def gelu_tanh(values):
    return jax.nn.gelu(values, approximate=True)

def reference(acts_prev, embedded, grads_next, loss_grad, up_weight, down_weight):
    factors = LEVELS + 1
    previous = acts_prev.reshape(N_SECTION, TOK, D)
    section_inputs = jnp.concatenate([embedded[None], previous[:-1]], axis=0)
    following = grads_next.reshape(N_SECTION, TOK, D)
    section_grads = jnp.concatenate([following[1:], loss_grad[None]], axis=0)
    per_device = DBLOCKS // N_TENSOR
    block_ids = jnp.arange(DBLOCKS, dtype=jnp.int32)
    tables = [block_ids]
    for level_idx in range(LEVELS):
        far = N_TENSOR >> LEVELS - level_idx
        tables.append((jnp.bitwise_xor(block_ids // per_device, far) * per_device + block_ids % per_device).astype(jnp.int32))
    anchor = (jnp.arange(HBLOCKS, dtype=jnp.int32) // EXPAND).astype(jnp.int32)

    def section_layer(operands):
        inputs, cotangent, up_section, down_section = operands
        inputs_f = inputs.astype(jnp.float32).reshape(TOK, DBLOCKS, BLK)
        grads_f = cotangent.astype(jnp.float32).reshape(TOK, DBLOCKS, BLK)
        up_f = up_section.astype(jnp.float32).reshape(factors, BLK, HBLOCKS, BLK)
        down_f = down_section.astype(jnp.float32).reshape(factors, HBLOCKS, BLK, BLK)
        seen_x = [inputs_f[:, table][:, anchor] for table in tables]
        seen_g = [grads_f[:, table][:, anchor] for table in tables]
        pre = jnp.zeros((TOK, HBLOCKS, BLK), jnp.float32)
        for factor in range(factors):
            pre = pre + jnp.einsum('tjp,pjq->tjq', seen_x[factor], up_f[factor])
        hidden = gelu_tanh(pre).astype(jnp.bfloat16)
        hidden_f = hidden.astype(jnp.float32)
        branch = jnp.zeros((TOK, DBLOCKS, BLK), jnp.float32)
        for factor in range(factors):
            part = jnp.einsum('tjp,jpq->tjq', hidden_f, down_f[factor]).reshape(TOK, DBLOCKS, EXPAND, BLK).sum(axis=2)
            if factor > 0:
                part = lax.optimization_barrier(part.astype(jnp.bfloat16)).astype(jnp.float32)[:, tables[factor]]
            branch = branch + part
        mixed = (inputs_f + branch).reshape(TOK, D).astype(jnp.bfloat16)
        grad_hidden = jnp.zeros((TOK, HBLOCKS, BLK), jnp.float32)
        down_grads = []
        for factor in range(factors):
            grad_hidden = grad_hidden + jnp.einsum('tjq,jpq->tjp', seen_g[factor], down_f[factor])
            down_grads.append(jnp.einsum('tjp,tjq->jpq', hidden_f, seen_g[factor]))
        down_grad = jnp.stack(down_grads).reshape(factors, H, BLK).astype(jnp.bfloat16)
        pullback = jax.vjp(gelu_tanh, pre)[1]
        grad_pre = pullback(grad_hidden)[0].astype(jnp.bfloat16).astype(jnp.float32)
        up_grads = []
        back_sum = grads_f
        for factor in range(factors):
            up_grads.append(jnp.einsum('tjp,tjq->pjq', seen_x[factor], grad_pre))
            back = jnp.einsum('tjq,pjq->tjp', grad_pre, up_f[factor]).reshape(TOK, DBLOCKS, EXPAND, BLK).sum(axis=2)
            if factor > 0:
                back = lax.optimization_barrier(back.astype(jnp.bfloat16)).astype(jnp.float32)[:, tables[factor]]
            back_sum = back_sum + back
        up_grad = jnp.stack(up_grads).reshape(factors, BLK, H).astype(jnp.bfloat16)
        input_grads = back_sum.reshape(TOK, D).astype(jnp.bfloat16)
        return (mixed, input_grads, up_grad, down_grad)
    mixed, input_grads, up_grad, down_grad = lax.map(section_layer, (section_inputs, section_grads, up_weight, down_weight))
    return (mixed.reshape(N_SECTION * TOK, D), input_grads.reshape(N_SECTION * TOK, D), up_grad, down_grad)
```

```python
import math

import jax
import jax.numpy as jnp
from jax import lax
from jax.experimental import pallas as pl
from jax.experimental.pallas import tpu as pltpu
from jax.sharding import PartitionSpec as P

TANH_SCALE = math.sqrt(2.0 / math.pi)
CUBIC = 0.044715
F32 = jnp.float32
BF16 = jnp.bfloat16


def shifted(value, by):
    length = lax.axis_size("section")
    pairs = [(i, i + by) for i in range(length) if 0 <= i + by < length]
    return lax.ppermute(value, "section", pairs)


def swapped(value, mask):
    pairs = [(source, source ^ mask) for source in range(lax.axis_size("tensor"))]
    return lax.ppermute(value, "tensor", pairs)


def mm(a, b, contract):
    return lax.dot_general(a, b, ((contract[:1], contract[1:]), ((), ())), preferred_element_type=F32)


def rows_of(refs):
    return jnp.concatenate([ref[...] for ref in refs], axis=0)


def pick(edge, if_edge, otherwise, start, rows, after=()):
    columns = if_edge.shape[1]

    def kernel(a, b, *rest):
        at_edge = lax.axis_index("section") == edge
        rest[-1][...] = jnp.where(at_edge, rows_at(a), rows_at(b))

    def rows_at(ref):
        at = 0 if ref.shape[0] == rows else start
        return ref[at : at + rows, :]

    vmem = pl.BlockSpec(memory_space=pltpu.VMEM)
    return pl.pallas_call(
        kernel,
        in_specs=[vmem, vmem] + [pl.BlockSpec(memory_space=pl.ANY)] * len(after),
        out_specs=vmem,
        out_shape=jax.ShapeDtypeStruct((rows, columns), if_edge.dtype),
        compiler_params=pltpu.CompilerParams(vmem_limit_bytes=8 * 2**20),
        cost_estimate=pl.CostEstimate(flops=0, bytes_accessed=0, transcendentals=0),
    )(if_edge, otherwise, *after)


def cut(wanted, args):
    columns = args[0].shape[1]

    def kernel(*refs):
        sources, outs, sems = refs[: len(args)], refs[len(args) : -1], refs[-1]
        section = lax.axis_index("section")
        for i, (edge, there, elsewhere, start, rows) in enumerate(wanted):
            piece = pl.ds(start, rows)
            if there != elsewhere:

                @pl.when(section == edge)
                def _():
                    pltpu.make_async_copy(sources[there].at[piece], outs[i], sems.at[i]).start()

                @pl.when(section != edge)
                def _():
                    pltpu.make_async_copy(sources[elsewhere].at[piece], outs[i], sems.at[i]).start()

            else:
                pltpu.make_async_copy(sources[there].at[piece], outs[i], sems.at[i]).start()
        for i, (_, there, _, start, rows) in enumerate(wanted):
            pltpu.make_async_copy(sources[there].at[pl.ds(start, rows)], outs[i], sems.at[i]).wait()

    return pl.pallas_call(
        kernel,
        in_specs=[pl.BlockSpec(memory_space=pl.ANY)] * len(args),
        out_specs=[pl.BlockSpec(memory_space=pltpu.VMEM)] * len(wanted),
        out_shape=[jax.ShapeDtypeStruct((w[4], columns), args[0].dtype) for w in wanted],
        scratch_shapes=[pltpu.SemaphoreType.DMA((len(wanted),))],
        cost_estimate=pl.CostEstimate(flops=0, bytes_accessed=0, transcendentals=0),
    )(*args)


def behind(value, other):
    return lax.optimization_barrier((value, other))[0]


def gate(v):
    return jnp.tanh(TANH_SCALE * (v + CUBIC * (v * v * v)))


def split(refs, counts):
    groups = []
    for count in counts:
        groups.append(refs[:count])
        refs = refs[count:]
    return groups + [refs]


def forward_kernel(counts, expand, *refs):
    own, theirs, rest = split(refs, counts)
    up, down, base, sent = rest[:2] + rest[-2:]
    width = up.shape[1]
    x = jnp.concatenate([rows_of(own), rows_of(theirs)], axis=1)
    kept = x[:, :width].astype(F32)
    away = jnp.zeros((x.shape[0], width), F32)
    for e in range(expand):
        block = slice(e * width, (e + 1) * width)
        pre = mm(x, up[:, :, block].reshape(2 * width, width), (1, 0))
        hidden = (0.5 * pre * (1.0 + gate(pre))).astype(BF16)
        kept = kept + mm(hidden, down[0, block, :], (1, 0))
        away = away + mm(hidden, down[1, block, :], (1, 0))
    base[...] = kept
    sent[...] = away.astype(BF16)


def backward_kernel(counts, expand, *refs):
    own_x, their_x, own_g, their_g, rest = split(refs, counts)
    up, down, base, sent, up_grad, down_grad = rest[:2] + rest[-4:]
    width = up.shape[1]
    x = jnp.concatenate([rows_of(own_x), rows_of(their_x)], axis=1)
    g = jnp.concatenate([rows_of(own_g), rows_of(their_g)], axis=1)
    kept = g[:, :width].astype(F32)
    away = jnp.zeros((x.shape[0], width), F32)
    for e in range(expand):
        block = slice(e * width, (e + 1) * width)
        up_block = up[:, :, block].reshape(2 * width, width)
        pre = mm(x, up_block, (1, 0))
        grad_hidden = mm(g[:, :width], down[0, block, :], (1, 1)) + mm(
            g[:, width:], down[1, block, :], (1, 1)
        )
        t = gate(pre)
        half = 0.5 * (1.0 + t)
        hidden = (pre * half).astype(BF16)
        slope = half + 0.5 * pre * (1.0 - t * t) * (
            TANH_SCALE * (1.0 + 3.0 * CUBIC * (pre * pre))
        )
        grad_pre = (grad_hidden * slope).astype(BF16)
        kept = kept + mm(grad_pre, up[0, :, block], (1, 1))
        away = away + mm(grad_pre, up[1, :, block], (1, 1))
        down_step = mm(hidden, g, (0, 0)).astype(BF16)
        down_grad[0, block, :] = down_step[:, :width]
        down_grad[1, block, :] = down_step[:, width:]
        up_step = mm(x, grad_pre, (0, 0)).astype(BF16)
        up_grad[0, :, block] = up_step[:width]
        up_grad[1, :, block] = up_step[width:]
    base[...] = kept
    sent[...] = away.astype(BF16)


def specs_of(arrays, width):
    return [pl.BlockSpec((a.shape[0], width), lambda m: (0, m)) for a in arrays]


def weight_specs(up, down, model_local):
    factors, width, hidden = up.shape
    per = hidden // model_local
    return [
        pl.BlockSpec((factors, width, per), lambda m: (0, 0, m)),
        pl.BlockSpec((factors, per, width), lambda m: (0, m, 0)),
    ]


def run(kernel, rows, weights, with_grads, products, after):
    up, down = weights
    factors, width, hidden = up.shape
    flat = [a for group in rows for a in group]
    tokens = sum(a.shape[0] for a in rows[0])
    columns = flat[0].shape[1]
    model_local = columns // width
    expand = hidden // columns
    w_specs = weight_specs(up, down, model_local)
    out_shape = [
        jax.ShapeDtypeStruct((tokens, columns), F32),
        jax.ShapeDtypeStruct((tokens, columns), BF16),
    ]
    out_specs = [pl.BlockSpec((tokens, width), lambda m: (0, m))] * 2
    if with_grads:
        out_shape += [jax.ShapeDtypeStruct(w.shape, BF16) for w in weights]
        out_specs += w_specs
    macs = products * factors * tokens * width * hidden
    return pl.pallas_call(
        lambda *refs: kernel([len(group) for group in rows], expand, *refs),
        grid=(model_local,),
        in_specs=specs_of(flat, width)
        + w_specs
        + [pl.BlockSpec(memory_space=pl.ANY)] * len(after),
        out_specs=out_specs,
        out_shape=out_shape,
        compiler_params=pltpu.CompilerParams(vmem_limit_bytes=32 * 2**20),
        cost_estimate=pl.CostEstimate(
            flops=200 * macs,
            bytes_accessed=4 * (up.size + down.size) + 8 * tokens * columns,
            transcendentals=tokens * hidden,
        ),
    )(*flat, *weights, *after)


def on_device(acts_prev, embedded, grads_next, loss_grad, up_weight, down_weight):
    up, down = up_weight[0], down_weight[0]
    levels = up.shape[0] - 1
    mask = lax.axis_size("tensor") >> levels
    tokens = acts_prev.shape[0]
    end = tokens * 3 // 4
    middle = end // 2
    first, last = 0, lax.axis_size("section") - 1

    early_x, cut_a, early_g, cut_b, cut_c = cut(
        [
            (last, 3, 0, end, tokens - end),
            (first, 0, 0, 0, middle),
            (first, 1, 2, end, tokens - end),
            (first, 0, 0, middle, end - middle),
            (first, 0, 0, end, tokens - end),
        ],
        (acts_prev, embedded, grads_next, loss_grad),
    )
    early_x = swapped(early_x, mask)
    came_a = shifted(cut_a, 1)
    early_g = swapped(early_g, mask)
    came_g = shifted(behind(grads_next, cut_a), -1)
    came_b = shifted(behind(cut_b, early_x), 1)
    own_a = pick(first, embedded, came_a, 0, middle)
    their_a = swapped(own_a, mask)
    came_c = shifted(behind(cut_c, early_g), 1)
    own_b = pick(first, embedded, came_b, middle, end - middle, (own_a,))
    their_b = swapped(own_b, mask)
    own_c = pick(first, embedded, came_c, end, tokens - end)
    own_g = pick(last, loss_grad, came_g, 0, tokens, (own_b,))
    sent_g = own_g[:end]
    their_g = swapped(sent_g, mask)
    their_c = pick(first, early_g, shifted(early_x, 1), 0, tokens - end)
    their_g_c = pick(last, early_x, shifted(early_g, -1), 0, tokens - end)
    own_x, their_x = [own_a, own_b, own_c], [their_a, their_b, their_c]
    their_g = [their_g, their_g_c]

    base_out, sent_out = run(
        forward_kernel, (own_x, their_x), (up, down), False, 2, (sent_g,)
    )
    arrived_out = swapped(sent_out, mask)
    base_back, sent_back, up_grad, down_grad = run(
        backward_kernel, (own_x, their_x, [own_g], their_g), (up, down), True, 5, (sent_out,)
    )
    arrived_back = swapped(sent_back, mask)
    mixed = (base_out + arrived_out.astype(F32)).astype(BF16)
    input_grads = (base_back + arrived_back.astype(F32)).astype(BF16)
    return (mixed, input_grads, up_grad[None], down_grad[None])


def solution(mesh):
    in_specs = (
        P("section", "tensor"),
        P(None, "tensor"),
        P("section", "tensor"),
        P(None, "tensor"),
        P("section", None, None, "tensor"),
        P("section", None, "tensor", None),
    )
    out_specs = (
        P("section", "tensor"),
        P("section", "tensor"),
        P("section", None, None, "tensor"),
        P("section", None, "tensor", None),
    )
    return jax.shard_map(
        on_device, mesh=mesh, in_specs=in_specs, out_specs=out_specs, check_vma=False
    )
```

```python
import math

import jax
import jax.numpy as jnp
from jax import lax
from jax.experimental import pallas as pl
from jax.experimental.pallas import tpu as pltpu
from jax.sharding import PartitionSpec as P

EARLY = 224
BYTES = 0
COST_A = 6
COST_J = 2 * 10**9
COST_C = 0
COST_B = 10
TANH_SCALE = math.sqrt(2.0 / math.pi)
CUBIC = 0.044715
F32 = jnp.float32
BF16 = jnp.bfloat16


def shifted(value, by):
    length = lax.axis_size("section")
    pairs = [(i, i + by) for i in range(length) if 0 <= i + by < length]
    return lax.ppermute(value, "section", pairs)


def swapped(value, mask):
    pairs = [(source, source ^ mask) for source in range(lax.axis_size("tensor"))]
    return lax.ppermute(value, "tensor", pairs)


def mm(a, b, contract):
    return lax.dot_general(a, b, ((contract[:1], contract[1:]), ((), ())), preferred_element_type=F32)


def rows_of(refs):
    return jnp.concatenate([ref[...] for ref in refs], axis=0)


def pick(edge, at_edge, elsewhere, rows, after=(), sent=0):
    (one, one_start), (other, other_start) = at_edge, elsewhere
    columns = one.shape[1]
    sizes = [rows, sent] if sent else [rows]

    def kernel(a, b, *rest):
        there = lax.axis_index("section") == edge
        value = jnp.where(there, a[one_start : one_start + rows, :], b[other_start : other_start + rows, :])
        for size, out in zip(sizes, rest[len(after) :]):
            out[...] = value[:size]

    vmem = pl.BlockSpec(memory_space=pltpu.VMEM)
    outs = pl.pallas_call(
        kernel,
        in_specs=[vmem, vmem] + [pl.BlockSpec(memory_space=pl.ANY)] * len(after),
        out_specs=[vmem] * len(sizes),
        out_shape=[jax.ShapeDtypeStruct((size, columns), one.dtype) for size in sizes],
        compiler_params=pltpu.CompilerParams(vmem_limit_bytes=8 * 2**20),
        cost_estimate=pl.CostEstimate(flops=0, bytes_accessed=0, transcendentals=0),
    )(one, other, *after)
    return outs if sent else outs[0]


def cut(outs_wanted, args):
    columns = args[0].shape[1]
    pieces = []
    for o, wanted in enumerate(outs_wanted):
        at = 0
        for edge, there, elsewhere, rows in wanted:
            pieces.append((o, at, edge, there, elsewhere, rows))
            at += rows

    def kernel(*refs):
        sources, outs, sems = refs[: len(args)], refs[len(args) : -1], refs[-1]
        section = lax.axis_index("section")

        def copy(i, which):
            o, at, rows = pieces[i][0], pieces[i][1], pieces[i][5]
            arg, start = pieces[i][which]
            return pltpu.make_async_copy(
                sources[arg].at[pl.ds(start, rows)], outs[o].at[pl.ds(at, rows)], sems.at[i]
            )

        for i, (_, _, edge, there, elsewhere, _) in enumerate(pieces):
            if there == elsewhere:
                copy(i, 3).start()
            else:
                pl.when(section == edge)(lambda i=i: copy(i, 3).start())
                pl.when(section != edge)(lambda i=i: copy(i, 4).start())
        for i in range(len(pieces)):
            copy(i, 3).wait()

    return pl.pallas_call(
        kernel,
        in_specs=[pl.BlockSpec(memory_space=pl.ANY)] * len(args),
        out_specs=[pl.BlockSpec(memory_space=pltpu.VMEM)] * len(outs_wanted),
        out_shape=[
            jax.ShapeDtypeStruct((sum(w[3] for w in wanted), columns), args[0].dtype)
            for wanted in outs_wanted
        ],
        scratch_shapes=[pltpu.SemaphoreType.DMA((len(pieces),))],
        cost_estimate=pl.CostEstimate(flops=0, bytes_accessed=0, transcendentals=0),
    )(*args)


def join(outs_wanted, args, after, cost=0):
    columns = args[0].shape[1]

    def kernel(*refs):
        for wanted, out in zip(outs_wanted, refs[len(args) + len(after) :]):
            at = 0
            for arg, start, rows in wanted:
                out[at : at + rows, :] = refs[arg][start : start + rows, :]
                at += rows

    vmem = pl.BlockSpec(memory_space=pltpu.VMEM)
    return pl.pallas_call(
        kernel,
        in_specs=[vmem] * len(args) + [pl.BlockSpec(memory_space=pl.ANY)] * len(after),
        out_specs=[vmem] * len(outs_wanted),
        out_shape=[
            jax.ShapeDtypeStruct((sum(w[2] for w in wanted), columns), args[0].dtype)
            for wanted in outs_wanted
        ],
        compiler_params=pltpu.CompilerParams(vmem_limit_bytes=8 * 2**20),
        cost_estimate=pl.CostEstimate(flops=cost, bytes_accessed=0, transcendentals=0),
    )(*args, *after)


def behind(value, other):
    return lax.optimization_barrier((value, other))[0]


def gate(v):
    return jnp.tanh(TANH_SCALE * (v + CUBIC * (v * v * v)))


def split(refs, counts):
    groups = []
    for count in counts:
        groups.append(refs[:count])
        refs = refs[count:]
    return groups + [refs]


def forward_kernel(counts, expand, *refs):
    own, theirs, rest = split(refs, counts)
    up, down, base, sent = rest[:2] + rest[-2:]
    width = up.shape[1]
    x = jnp.concatenate([rows_of(own), rows_of(theirs)], axis=1)
    kept = x[:, :width].astype(F32)
    away = jnp.zeros((x.shape[0], width), F32)
    for e in range(expand):
        block = slice(e * width, (e + 1) * width)
        pre = mm(x, up[:, :, block].reshape(2 * width, width), (1, 0))
        hidden = (0.5 * pre * (1.0 + gate(pre))).astype(BF16)
        kept = kept + mm(hidden, down[0, block, :], (1, 0))
        away = away + mm(hidden, down[1, block, :], (1, 0))
    base[...] = kept
    sent[...] = away.astype(BF16)


def backward_kernel(counts, expand, *refs):
    own_x, their_x, own_g, their_g, rest = split(refs, counts)
    up, down, base, sent, up_grad, down_grad = rest[:2] + rest[-4:]
    width = up.shape[1]
    x = jnp.concatenate([rows_of(own_x), rows_of(their_x)], axis=1)
    g = jnp.concatenate([rows_of(own_g), rows_of(their_g)], axis=1)
    kept = g[:, :width].astype(F32)
    away = jnp.zeros((x.shape[0], width), F32)
    for e in range(expand):
        block = slice(e * width, (e + 1) * width)
        up_block = up[:, :, block].reshape(2 * width, width)
        pre = mm(x, up_block, (1, 0))
        grad_hidden = mm(g[:, :width], down[0, block, :], (1, 1)) + mm(
            g[:, width:], down[1, block, :], (1, 1)
        )
        t = gate(pre)
        half = 0.5 * (1.0 + t)
        hidden = (pre * half).astype(BF16)
        slope = half + 0.5 * pre * (1.0 - t * t) * (
            TANH_SCALE * (1.0 + 3.0 * CUBIC * (pre * pre))
        )
        grad_pre = (grad_hidden * slope).astype(BF16)
        kept = kept + mm(grad_pre, up[0, :, block], (1, 1))
        away = away + mm(grad_pre, up[1, :, block], (1, 1))
        down_step = mm(hidden, g, (0, 0)).astype(BF16)
        down_grad[0, block, :] = down_step[:, :width]
        down_grad[1, block, :] = down_step[:, width:]
        up_step = mm(x, grad_pre, (0, 0)).astype(BF16)
        up_grad[0, :, block] = up_step[:width]
        up_grad[1, :, block] = up_step[width:]
    base[...] = kept
    sent[...] = away.astype(BF16)


def specs_of(arrays, width):
    return [pl.BlockSpec((a.shape[0], width), lambda m: (0, m)) for a in arrays]


def weight_specs(up, down, model_local):
    factors, width, hidden = up.shape
    per = hidden // model_local
    return [
        pl.BlockSpec((factors, width, per), lambda m: (0, 0, m)),
        pl.BlockSpec((factors, per, width), lambda m: (0, m, 0)),
    ]


def run(kernel, rows, weights, with_grads, weight, after):
    up, down = weights
    factors, width, hidden = up.shape
    flat = [a for group in rows for a in group]
    tokens = sum(a.shape[0] for a in rows[0])
    columns = flat[0].shape[1]
    model_local = columns // width
    expand = hidden // columns
    w_specs = weight_specs(up, down, model_local)
    out_shape = [
        jax.ShapeDtypeStruct((tokens, columns), F32),
        jax.ShapeDtypeStruct((tokens, columns), BF16),
    ]
    out_specs = [pl.BlockSpec((tokens, width), lambda m: (0, m))] * 2
    if with_grads:
        out_shape += [jax.ShapeDtypeStruct(w.shape, BF16) for w in weights]
        out_specs += w_specs
    macs = factors * tokens * width * hidden
    return pl.pallas_call(
        lambda *refs: kernel([len(group) for group in rows], expand, *refs),
        grid=(model_local,),
        in_specs=specs_of(flat, width)
        + w_specs
        + [pl.BlockSpec(memory_space=pl.ANY)] * len(after),
        out_specs=out_specs,
        out_shape=out_shape,
        compiler_params=pltpu.CompilerParams(vmem_limit_bytes=32 * 2**20),
        cost_estimate=pl.CostEstimate(
            flops=int(weight * macs),
            bytes_accessed=BYTES,
            transcendentals=0,
        ),
    )(*flat, *weights, *after)


def on_device(acts_prev, embedded, grads_next, loss_grad, up_weight, down_weight):
    up, down = up_weight[0], down_weight[0]
    levels = up.shape[0] - 1
    mask = lax.axis_size("tensor") >> levels
    tokens = acts_prev.shape[0]
    early = tokens * EARLY // 512 // 16 * 16
    end = tokens - early
    first, last = 0, lax.axis_size("section") - 1

    (crossing,) = cut(
        [[(last, (3, end), (0, end), early), (first, (1, end), (2, end), early)]],
        (acts_prev, embedded, grads_next, loss_grad),
    )
    crossed = swapped(crossing, mask)
    cut_a, cut_c = join([[(0, 0, end)], [(0, end, early)]], (acts_prev,), ())
    came_a = shifted(cut_a, 1)
    came_g = shifted(behind(grads_next, crossing), -1)
    own_a = pick(first, (embedded, 0), (came_a, 0), end)
    their_a = swapped(own_a, mask)
    onward_x, onward_g = join(
        [[(0, 0, early), (1, 0, early)], [(1, early, early)]], (cut_c, crossed), (own_a,), COST_J
    )
    came_c = shifted(onward_x, 1)
    came_g_c = shifted(onward_g, -1)
    own_g, sent_g = pick(last, (loss_grad, 0), (came_g, 0), tokens, (own_a, onward_g), end)
    their_g = swapped(sent_g, mask)
    base_a, sent_a = run(
        forward_kernel, ([own_a], [their_a]), (up, down), False, COST_A, (sent_g,)
    )
    arrived_a = swapped(sent_a, mask)
    own_c = pick(first, (embedded, end), (came_c, 0), early, (sent_a,))
    their_c = pick(first, (crossed, early), (came_c, early), early, (sent_a,))
    their_g_c = pick(last, (crossed, 0), (came_g_c, 0), early, (sent_a,))
    base_c, sent_c = run(forward_kernel, ([own_c], [their_c]), (up, down), False, COST_C, (sent_a,))
    arrived_c = swapped(sent_c, mask)
    base_out = jnp.concatenate([base_a, base_c])
    arrived_out = jnp.concatenate([arrived_a, arrived_c])
    own_x, their_x = [own_a, own_c], [their_a, their_c]
    their_g = [their_g, their_g_c]
    base_back, sent_back, up_grad, down_grad = run(
        backward_kernel, (own_x, their_x, [own_g], their_g), (up, down), True, COST_B, (sent_c,)
    )
    quarter = tokens // 4
    arrived_back = jnp.concatenate(
        [swapped(sent_back[i * quarter : (i + 1) * quarter], mask) for i in range(4)]
    )
    mixed = (base_out + arrived_out.astype(F32)).astype(BF16)
    base_back = behind(base_back, mixed)
    input_grads = (base_back + arrived_back.astype(F32)).astype(BF16)
    return (mixed, input_grads, up_grad[None], down_grad[None])


def solution(mesh):
    in_specs = (
        P("section", "tensor"),
        P(None, "tensor"),
        P("section", "tensor"),
        P(None, "tensor"),
        P("section", None, None, "tensor"),
        P("section", None, "tensor", None),
    )
    out_specs = (
        P("section", "tensor"),
        P("section", "tensor"),
        P("section", None, None, "tensor"),
        P("section", None, "tensor", None),
    )
    return jax.shard_map(
        on_device, mesh=mesh, in_specs=in_specs, out_specs=out_specs, check_vma=False
    )
```

```python
import math

import jax
import jax.numpy as jnp
from jax import lax
from jax.experimental import pallas as pl
from jax.experimental.pallas import tpu as pltpu
from jax.sharding import PartitionSpec as P

COST_A = 3 * 10**9
COST_G = 10**9
COST_B = 4 * 10**9
COST_BACK = 6 * 10**9
LIMIT = 8
BYTES = 8 * 2**20
TANH_SCALE = math.sqrt(2.0 / math.pi)
CUBIC = 0.044715
F32 = jnp.float32
BF16 = jnp.bfloat16


def shifted(value, by):
    length = lax.axis_size("section")
    pairs = [(i, i + by) for i in range(length) if 0 <= i + by < length]
    return lax.ppermute(value, "section", pairs)


def swapped(value, mask):
    pairs = [(source, source ^ mask) for source in range(lax.axis_size("tensor"))]
    return lax.ppermute(value, "tensor", pairs)


def exchanged(value, mask, sections):
    size = lax.axis_size("tensor")
    pairs = []
    for s in range(lax.axis_size("section")):
        distance = mask if s in sections else 1
        pairs += [(s * size + t, s * size + (t ^ distance)) for t in range(size)]
    return lax.ppermute(value, ("section", "tensor"), pairs)


def mm(a, b, contract):
    return lax.dot_general(a, b, ((contract[:1], contract[1:]), ((), ())), preferred_element_type=F32)


def rows_of(refs):
    return jnp.concatenate([ref[...] for ref in refs], axis=0)


def pick(edge, at_edge, elsewhere, rows, after=(), cost=0):
    (one, one_start), (other, other_start) = at_edge, elsewhere

    def kernel(a, b, *rest):
        there = lax.axis_index("section") == edge
        rest[-1][...] = jnp.where(
            there, a[one_start : one_start + rows, :], b[other_start : other_start + rows, :]
        )

    vmem = pl.BlockSpec(memory_space=pltpu.VMEM)
    return pl.pallas_call(
        kernel,
        in_specs=[vmem, vmem] + [pl.BlockSpec(memory_space=pl.ANY)] * len(after),
        out_specs=vmem,
        out_shape=jax.ShapeDtypeStruct((rows, one.shape[1]), one.dtype),
        compiler_params=pltpu.CompilerParams(vmem_limit_bytes=8 * 2**20),
        cost_estimate=pl.CostEstimate(flops=cost, bytes_accessed=0, transcendentals=0),
    )(one, other, *after)


def join(outs_wanted, args, after, cost=0):
    columns = args[0].shape[1]

    def kernel(*refs):
        for wanted, out in zip(outs_wanted, refs[len(args) + len(after) :]):
            at = 0
            for arg, start, rows in wanted:
                out[at : at + rows, :] = refs[arg][start : start + rows, :]
                at += rows

    vmem = pl.BlockSpec(memory_space=pltpu.VMEM)
    return pl.pallas_call(
        kernel,
        in_specs=[vmem] * len(args) + [pl.BlockSpec(memory_space=pl.ANY)] * len(after),
        out_specs=[vmem] * len(outs_wanted),
        out_shape=[
            jax.ShapeDtypeStruct((sum(w[2] for w in wanted), columns), args[0].dtype)
            for wanted in outs_wanted
        ],
        compiler_params=pltpu.CompilerParams(vmem_limit_bytes=8 * 2**20),
        cost_estimate=pl.CostEstimate(flops=cost, bytes_accessed=BYTES, transcendentals=0),
    )(*args, *after)


def gate(v):
    return jnp.tanh(TANH_SCALE * (v + CUBIC * (v * v * v)))


def split(refs, counts):
    groups = []
    for count in counts:
        groups.append(refs[:count])
        refs = refs[count:]
    return groups + [refs]


def columns_of(refs, block):
    return jnp.concatenate([ref[:, block] for ref in refs], axis=0)


def over_blocks(width, columns, expand, body):
    @pl.loop(0, columns // width)
    def _(m):
        model = pl.ds(pl.multiple_of(m * width, width), width)
        body(
            model,
            [pl.ds(pl.multiple_of((m * expand + e) * width, width), width) for e in range(expand)],
        )


def forward_kernel(counts, *refs):
    own, theirs, rest = split(refs, counts)
    up, down = rest[:2]
    base, sent = rest[-2:]
    width, columns = up.shape[1], base.shape[1]

    def body(model, blocks):
        x = jnp.concatenate([columns_of(own, model), columns_of(theirs, model)], axis=1)
        kept = x[:, :width].astype(F32)
        away = jnp.zeros((x.shape[0], width), F32)
        for block in blocks:
            pre = mm(x, up[:, :, block].reshape(2 * width, width), (1, 0))
            hidden = (0.5 * pre * (1.0 + gate(pre))).astype(BF16)
            kept = kept + mm(hidden, down[0, block, :], (1, 0))
            away = away + mm(hidden, down[1, block, :], (1, 0))
        base[:, model] = kept
        sent[:, model] = away.astype(BF16)

    over_blocks(width, columns, up.shape[2] // columns, body)


def backward_kernel(counts, *refs):
    own_x, their_x, own_g, their_g, rest = split(refs, counts)
    up, down = rest[:2]
    base, sent, hidden_out, grad_pre_out = rest[-4:]
    width, columns = up.shape[1], base.shape[1]

    def body(model, blocks):
        x = jnp.concatenate([columns_of(own_x, model), columns_of(their_x, model)], axis=1)
        own, theirs = columns_of(own_g, model), columns_of(their_g, model)
        kept = own.astype(F32)
        away = jnp.zeros((x.shape[0], width), F32)
        for block in blocks:
            pre = mm(x, up[:, :, block].reshape(2 * width, width), (1, 0))
            grad_hidden = mm(own, down[0, block, :], (1, 1)) + mm(theirs, down[1, block, :], (1, 1))
            t = gate(pre)
            half = 0.5 * (1.0 + t)
            slope = half + 0.5 * pre * (1.0 - t * t) * (
                TANH_SCALE * (1.0 + 3.0 * CUBIC * (pre * pre))
            )
            grad_pre = (grad_hidden * slope).astype(BF16)
            kept = kept + mm(grad_pre, up[0, :, block], (1, 1))
            away = away + mm(grad_pre, up[1, :, block], (1, 1))
            hidden_out[:, block] = (pre * half).astype(BF16)
            grad_pre_out[:, block] = grad_pre
        base[:, model] = kept
        sent[:, model] = away.astype(BF16)

    over_blocks(width, columns, up.shape[2] // columns, body)


def in_vmem(kernel, rows, others, outs, cost, after=()):
    flat = [a for group in rows for a in group]
    vmem = pl.BlockSpec(memory_space=pltpu.VMEM)
    return pl.pallas_call(
        lambda *refs: kernel([len(group) for group in rows], *refs),
        in_specs=[vmem] * (len(flat) + len(others))
        + [pl.BlockSpec(memory_space=pl.ANY)] * len(after),
        out_specs=[vmem] * len(outs),
        out_shape=outs,
        compiler_params=pltpu.CompilerParams(vmem_limit_bytes=LIMIT * 2**20),
        cost_estimate=pl.CostEstimate(flops=cost, bytes_accessed=0, transcendentals=0),
    )(*flat, *others, *after)


def load(args, after=()):
    def kernel(*refs):
        sems = refs[-1]
        copies = [
            pltpu.make_async_copy(refs[i], refs[len(args) + len(after) + i], sems.at[i])
            for i in range(len(args))
        ]
        for copy in copies:
            copy.start()
        for copy in copies:
            copy.wait()

    return pl.pallas_call(
        kernel,
        in_specs=[pl.BlockSpec(memory_space=pl.ANY)] * (len(args) + len(after)),
        out_specs=[pl.BlockSpec(memory_space=pltpu.VMEM)] * len(args),
        out_shape=[jax.ShapeDtypeStruct(a.shape, a.dtype) for a in args],
        scratch_shapes=[pltpu.SemaphoreType.DMA((len(args),))],
        compiler_params=pltpu.CompilerParams(vmem_limit_bytes=2 * 2**20),
        cost_estimate=pl.CostEstimate(flops=0, bytes_accessed=0, transcendentals=0),
    )(*args, *after)


def weight_kernel(counts, expand, *refs):
    own_x, their_x, own_g, their_g, rest = split(refs, counts)
    hidden, grad_pre = rest[:2]
    up_grad, down_grad = rest[-2:]
    width = up_grad.shape[1]
    x = jnp.concatenate([rows_of(own_x), rows_of(their_x)], axis=1)
    g = jnp.concatenate([rows_of(own_g), rows_of(their_g)], axis=1)
    for e in range(expand):
        block = slice(e * width, (e + 1) * width)
        down_step = mm(hidden[:, block], g, (0, 0)).astype(BF16)
        down_grad[0, block, :] = down_step[:, :width]
        down_grad[1, block, :] = down_step[:, width:]
        up_step = mm(x, grad_pre[:, block], (0, 0)).astype(BF16)
        up_grad[0, :, block] = up_step[:width]
        up_grad[1, :, block] = up_step[width:]


def run(kernel, rows, others, outs, width, cost, after=()):
    flat = [a for group in rows for a in group]
    model_local = flat[0].shape[1] // width

    def spec(a):
        if len(a.shape) == 2:
            return pl.BlockSpec((a.shape[0], a.shape[1] // model_local), lambda m: (0, m))
        if a.shape[2] == width:
            return pl.BlockSpec((a.shape[0], a.shape[1] // model_local, width), lambda m: (0, m, 0))
        return pl.BlockSpec((a.shape[0], width, a.shape[2] // model_local), lambda m: (0, 0, m))

    expand = max(max(a.shape) for a in others) // (width * model_local)
    return pl.pallas_call(
        lambda *refs: kernel([len(group) for group in rows], expand, *refs),
        grid=(model_local,),
        in_specs=[spec(a) for a in (*flat, *others)]
        + [pl.BlockSpec(memory_space=pl.ANY)] * len(after),
        out_specs=[spec(a) for a in outs],
        out_shape=outs,
        compiler_params=pltpu.CompilerParams(vmem_limit_bytes=20 * 2**20),
        cost_estimate=pl.CostEstimate(flops=cost, bytes_accessed=BYTES, transcendentals=0),
    )(*flat, *others, *after)


def finish(base, pieces, start, total, result=None, after=()):
    rows, columns = base.shape

    def kernel(*refs):
        base_ref, piece_refs = refs[0], refs[1 : 1 + len(pieces)]
        out, rounded, sem = refs[-3:]
        rounded[...] = (base_ref[...] + rows_of(piece_refs).astype(F32)).astype(BF16)
        copy = pltpu.make_async_copy(rounded, out.at[pl.ds(start, rows)], sem)
        copy.start()
        copy.wait()

    vmem, anywhere = pl.BlockSpec(memory_space=pltpu.VMEM), pl.BlockSpec(memory_space=pl.ANY)
    rest = after if result is None else (result, *after)
    return pl.pallas_call(
        kernel,
        in_specs=[vmem] * (1 + len(pieces)) + [anywhere] * len(rest),
        out_specs=anywhere,
        out_shape=jax.ShapeDtypeStruct((total, columns), BF16),
        scratch_shapes=[pltpu.VMEM((rows, columns), BF16), pltpu.SemaphoreType.DMA],
        input_output_aliases={} if result is None else {1 + len(pieces): 0},
        compiler_params=pltpu.CompilerParams(vmem_limit_bytes=8 * 2**20),
        cost_estimate=pl.CostEstimate(flops=0, bytes_accessed=0, transcendentals=0),
    )(base, *pieces, *rest)


def on_device(acts_prev, embedded, grads_next, loss_grad, up_weight, down_weight):
    up, down = up_weight[0], down_weight[0]
    levels = up.shape[0] - 1
    mask = lax.axis_size("tensor") >> levels
    factors, width, hidden_local = up.shape
    tokens, columns = acts_prev.shape
    half, quarter = tokens // 2, tokens // 4
    sections = lax.axis_size("section")
    first, last = 0, sections - 1

    crossed_g = exchanged(grads_next, mask, range(1, sections))
    crossed_loss = exchanged(loss_grad, mask, range(1))
    acts_a, acts_b = join([[(0, 0, half)], [(0, half, tokens - half)]], (acts_prev,), ())
    came_a = shifted(acts_a, 1)
    came_b = shifted(acts_b, 1)
    came_g = shifted(grads_next, -1)
    up, embedded = load((up, embedded), (acts_a,))
    own_a = pick(first, (embedded, 0), (came_a, 0), half)
    their_a = swapped(own_a, mask)
    down, loss_grad = load((down, loss_grad), (own_a,))
    own_b = pick(first, (embedded, half), (came_b, 0), tokens - half, (down,))
    their_b = swapped(own_b, mask)
    onward_g = lax.ppermute(
        pick(first, (crossed_loss, 0), (crossed_g, 0), tokens, (own_b,)),
        "section",
        [(s, (s - 1) % sections) for s in range(sections)],
    )
    own_g = pick(last, (loss_grad, 0), (came_g, 0), tokens, (own_b,), COST_G)

    def forward(own, theirs, cost, after):
        shape = own.shape
        return in_vmem(
            forward_kernel,
            ([own], [theirs]),
            (up, down),
            [jax.ShapeDtypeStruct(shape, F32), jax.ShapeDtypeStruct(shape, BF16)],
            cost,
            after,
        )

    base_a, sent_a = forward(own_a, their_a, COST_A, (own_b, own_g))
    arrived_a = swapped(sent_a, mask)
    base_b, sent_b = forward(own_b, their_b, COST_B, (sent_a,))
    arrived_b = swapped(sent_b, mask)
    rows = ([own_a, own_b], [their_a, their_b], [own_g], [onward_g])
    base_back, sent_back, hidden, grad_pre = in_vmem(
        backward_kernel,
        rows,
        (up, down),
        [
            jax.ShapeDtypeStruct((tokens, columns), F32),
            jax.ShapeDtypeStruct((tokens, columns), BF16),
            jax.ShapeDtypeStruct((tokens, hidden_local), BF16),
            jax.ShapeDtypeStruct((tokens, hidden_local), BF16),
        ],
        COST_BACK,
        (sent_b,),
    )
    arrived_back = [
        swapped(sent_back[i * quarter : (i + 1) * quarter], mask) for i in range(4)
    ]
    up_grad, down_grad = run(
        weight_kernel,
        rows,
        (hidden, grad_pre),
        [jax.ShapeDtypeStruct(w.shape, BF16) for w in (up, down)],
        width,
        0,
    )
    mixed = finish(base_a, [arrived_a], 0, tokens, None, (up_grad,))
    mixed = finish(base_b, [arrived_b], half, tokens, mixed)
    end = 3 * quarter
    input_grads = finish(base_back[:end], arrived_back[:3], 0, tokens, None, (mixed,))
    input_grads = finish(base_back[end:], arrived_back[3:], end, tokens, input_grads)
    return (mixed, input_grads, up_grad[None], down_grad[None])


def solution(mesh):
    in_specs = (
        P("section", "tensor"),
        P(None, "tensor"),
        P("section", "tensor"),
        P(None, "tensor"),
        P("section", None, None, "tensor"),
        P("section", None, "tensor", None),
    )
    out_specs = (
        P("section", "tensor"),
        P("section", "tensor"),
        P("section", None, None, "tensor"),
        P("section", None, "tensor", None),
    )
    return jax.shard_map(
        on_device, mesh=mesh, in_specs=in_specs, out_specs=out_specs, check_vma=False
    )
```

```python
import math

import jax
import jax.numpy as jnp
from jax import lax
from jax.experimental import pallas as pl
from jax.experimental.pallas import tpu as pltpu
from jax.sharding import PartitionSpec as P

COST_A = 3 * 10**9
COST_G = 10**9
COST_B = 7 * 10**9
COST_BACK = 6 * 10**9
LIMIT = 8
BYTES = 8 * 2**20
TANH_SCALE = math.sqrt(2.0 / math.pi)
CUBIC = 0.044715
F32 = jnp.float32
BF16 = jnp.bfloat16


def shifted(value, by):
    length = lax.axis_size("section")
    pairs = [(i, i + by) for i in range(length) if 0 <= i + by < length]
    return lax.ppermute(value, "section", pairs)


def swapped(value, mask):
    pairs = [(source, source ^ mask) for source in range(lax.axis_size("tensor"))]
    return lax.ppermute(value, "tensor", pairs)


def exchanged(value, mask, sections):
    size = lax.axis_size("tensor")
    pairs = []
    for s in range(lax.axis_size("section")):
        distance = mask if s in sections else 1
        pairs += [(s * size + t, s * size + (t ^ distance)) for t in range(size)]
    return lax.ppermute(value, ("section", "tensor"), pairs)


def mm(a, b, contract):
    return lax.dot_general(a, b, ((contract[:1], contract[1:]), ((), ())), preferred_element_type=F32)


def rows_of(refs):
    return jnp.concatenate([ref[...] for ref in refs], axis=0)


def pick(edge, at_edge, elsewhere, rows, after=(), cost=0):
    (one, one_start), (other, other_start) = at_edge, elsewhere

    def kernel(a, b, *rest):
        there = lax.axis_index("section") == edge
        rest[-1][...] = jnp.where(
            there, a[one_start : one_start + rows, :], b[other_start : other_start + rows, :]
        )

    vmem = pl.BlockSpec(memory_space=pltpu.VMEM)
    return pl.pallas_call(
        kernel,
        in_specs=[vmem, vmem] + [pl.BlockSpec(memory_space=pl.ANY)] * len(after),
        out_specs=vmem,
        out_shape=jax.ShapeDtypeStruct((rows, one.shape[1]), one.dtype),
        compiler_params=pltpu.CompilerParams(vmem_limit_bytes=8 * 2**20),
        cost_estimate=pl.CostEstimate(flops=cost, bytes_accessed=0, transcendentals=0),
    )(one, other, *after)


def join(outs_wanted, args, after, cost=0):
    columns = args[0].shape[1]

    def kernel(*refs):
        for wanted, out in zip(outs_wanted, refs[len(args) + len(after) :]):
            at = 0
            for arg, start, rows in wanted:
                out[at : at + rows, :] = refs[arg][start : start + rows, :]
                at += rows

    vmem = pl.BlockSpec(memory_space=pltpu.VMEM)
    return pl.pallas_call(
        kernel,
        in_specs=[vmem] * len(args) + [pl.BlockSpec(memory_space=pl.ANY)] * len(after),
        out_specs=[vmem] * len(outs_wanted),
        out_shape=[
            jax.ShapeDtypeStruct((sum(w[2] for w in wanted), columns), args[0].dtype)
            for wanted in outs_wanted
        ],
        compiler_params=pltpu.CompilerParams(vmem_limit_bytes=8 * 2**20),
        cost_estimate=pl.CostEstimate(flops=cost, bytes_accessed=BYTES, transcendentals=0),
    )(*args, *after)


def gate(v):
    return jnp.tanh(TANH_SCALE * (v + CUBIC * (v * v * v)))


def split(refs, counts):
    groups = []
    for count in counts:
        groups.append(refs[:count])
        refs = refs[count:]
    return groups + [refs]


def columns_of(refs, block):
    return jnp.concatenate([ref[:, block] for ref in refs], axis=0)


def over_blocks(width, columns, expand, body):
    @pl.loop(0, columns // width)
    def _(m):
        model = pl.ds(pl.multiple_of(m * width, width), width)
        body(
            model,
            [pl.ds(pl.multiple_of((m * expand + e) * width, width), width) for e in range(expand)],
        )


def forward_kernel(counts, *refs):
    own, theirs, rest = split(refs, counts)
    up, down = rest[:2]
    base, sent = rest[-2:]
    width, columns = up.shape[1], base.shape[1]

    def body(model, blocks):
        x = jnp.concatenate([columns_of(own, model), columns_of(theirs, model)], axis=1)
        kept = x[:, :width].astype(F32)
        away = jnp.zeros((x.shape[0], width), F32)
        for block in blocks:
            pre = mm(x, up[:, :, block].reshape(2 * width, width), (1, 0))
            hidden = (0.5 * pre * (1.0 + gate(pre))).astype(BF16)
            kept = kept + mm(hidden, down[0, block, :], (1, 0))
            away = away + mm(hidden, down[1, block, :], (1, 0))
        base[:, model] = kept
        sent[:, model] = away.astype(BF16)

    over_blocks(width, columns, up.shape[2] // columns, body)


def backward_kernel(counts, *refs):
    own_x, their_x, own_g, their_g, rest = split(refs, counts)
    up, down = rest[:2]
    base, sent, hidden_out, grad_pre_out = rest[-4:]
    width, columns = up.shape[1], base.shape[1]

    def body(model, blocks):
        x = jnp.concatenate([columns_of(own_x, model), columns_of(their_x, model)], axis=1)
        own, theirs = columns_of(own_g, model), columns_of(their_g, model)
        kept = own.astype(F32)
        away = jnp.zeros((x.shape[0], width), F32)
        for block in blocks:
            pre = mm(x, up[:, :, block].reshape(2 * width, width), (1, 0))
            grad_hidden = mm(own, down[0, block, :], (1, 1)) + mm(theirs, down[1, block, :], (1, 1))
            t = gate(pre)
            half = 0.5 * (1.0 + t)
            slope = half + 0.5 * pre * (1.0 - t * t) * (
                TANH_SCALE * (1.0 + 3.0 * CUBIC * (pre * pre))
            )
            grad_pre = (grad_hidden * slope).astype(BF16)
            kept = kept + mm(grad_pre, up[0, :, block], (1, 1))
            away = away + mm(grad_pre, up[1, :, block], (1, 1))
            hidden_out[:, block] = (pre * half).astype(BF16)
            grad_pre_out[:, block] = grad_pre
        base[:, model] = kept
        sent[:, model] = away.astype(BF16)

    over_blocks(width, columns, up.shape[2] // columns, body)


def in_vmem(kernel, rows, others, outs, cost, after=()):
    flat = [a for group in rows for a in group]
    vmem = pl.BlockSpec(memory_space=pltpu.VMEM)
    return pl.pallas_call(
        lambda *refs: kernel([len(group) for group in rows], *refs),
        in_specs=[vmem] * (len(flat) + len(others))
        + [pl.BlockSpec(memory_space=pl.ANY)] * len(after),
        out_specs=[vmem] * len(outs),
        out_shape=outs,
        compiler_params=pltpu.CompilerParams(vmem_limit_bytes=LIMIT * 2**20),
        cost_estimate=pl.CostEstimate(flops=cost, bytes_accessed=0, transcendentals=0),
    )(*flat, *others, *after)


def load(args, after=()):
    def kernel(*refs):
        sems = refs[-1]
        copies = [
            pltpu.make_async_copy(refs[i], refs[len(args) + len(after) + i], sems.at[i])
            for i in range(len(args))
        ]
        for copy in copies:
            copy.start()
        for copy in copies:
            copy.wait()

    return pl.pallas_call(
        kernel,
        in_specs=[pl.BlockSpec(memory_space=pl.ANY)] * (len(args) + len(after)),
        out_specs=[pl.BlockSpec(memory_space=pltpu.VMEM)] * len(args),
        out_shape=[jax.ShapeDtypeStruct(a.shape, a.dtype) for a in args],
        scratch_shapes=[pltpu.SemaphoreType.DMA((len(args),))],
        compiler_params=pltpu.CompilerParams(vmem_limit_bytes=2 * 2**20),
        cost_estimate=pl.CostEstimate(flops=0, bytes_accessed=0, transcendentals=0),
    )(*args, *after)


def weight_kernel(counts, expand, *refs):
    own_x, their_x, own_g, their_g, rest = split(refs, counts)
    hidden, grad_pre = rest[:2]
    up_grad, down_grad = rest[-2:]
    width = up_grad.shape[1]
    x = jnp.concatenate([rows_of(own_x), rows_of(their_x)], axis=1)
    g = jnp.concatenate([rows_of(own_g), rows_of(their_g)], axis=1)
    for e in range(expand):
        block = slice(e * width, (e + 1) * width)
        down_step = mm(hidden[:, block], g, (0, 0)).astype(BF16)
        down_grad[0, block, :] = down_step[:, :width]
        down_grad[1, block, :] = down_step[:, width:]
        up_step = mm(x, grad_pre[:, block], (0, 0)).astype(BF16)
        up_grad[0, :, block] = up_step[:width]
        up_grad[1, :, block] = up_step[width:]


def run(kernel, rows, others, outs, width, cost, after=()):
    flat = [a for group in rows for a in group]
    model_local = flat[0].shape[1] // width

    def spec(a):
        if len(a.shape) == 2:
            return pl.BlockSpec((a.shape[0], a.shape[1] // model_local), lambda m: (0, m))
        if a.shape[2] == width:
            return pl.BlockSpec((a.shape[0], a.shape[1] // model_local, width), lambda m: (0, m, 0))
        return pl.BlockSpec((a.shape[0], width, a.shape[2] // model_local), lambda m: (0, 0, m))

    expand = max(max(a.shape) for a in others) // (width * model_local)
    return pl.pallas_call(
        lambda *refs: kernel([len(group) for group in rows], expand, *refs),
        grid=(model_local,),
        in_specs=[spec(a) for a in (*flat, *others)]
        + [pl.BlockSpec(memory_space=pl.ANY)] * len(after),
        out_specs=[spec(a) for a in outs],
        out_shape=outs,
        compiler_params=pltpu.CompilerParams(vmem_limit_bytes=20 * 2**20),
        cost_estimate=pl.CostEstimate(flops=cost, bytes_accessed=BYTES, transcendentals=0),
    )(*flat, *others, *after)


def finish(base, pieces, start, total, result=None, after=()):
    rows, columns = base.shape

    def kernel(*refs):
        base_ref, piece_refs = refs[0], refs[1 : 1 + len(pieces)]
        out, rounded, sem = refs[-3:]
        rounded[...] = (base_ref[...] + rows_of(piece_refs).astype(F32)).astype(BF16)
        copy = pltpu.make_async_copy(rounded, out.at[pl.ds(start, rows)], sem)
        copy.start()
        copy.wait()

    vmem, anywhere = pl.BlockSpec(memory_space=pltpu.VMEM), pl.BlockSpec(memory_space=pl.ANY)
    rest = after if result is None else (result, *after)
    return pl.pallas_call(
        kernel,
        in_specs=[vmem] * (1 + len(pieces)) + [anywhere] * len(rest),
        out_specs=anywhere,
        out_shape=jax.ShapeDtypeStruct((total, columns), BF16),
        scratch_shapes=[pltpu.VMEM((rows, columns), BF16), pltpu.SemaphoreType.DMA],
        input_output_aliases={} if result is None else {1 + len(pieces): 0},
        compiler_params=pltpu.CompilerParams(vmem_limit_bytes=8 * 2**20),
        cost_estimate=pl.CostEstimate(flops=0, bytes_accessed=0, transcendentals=0),
    )(base, *pieces, *rest)


def on_device(acts_prev, embedded, grads_next, loss_grad, up_weight, down_weight):
    up, down = up_weight[0], down_weight[0]
    levels = up.shape[0] - 1
    mask = lax.axis_size("tensor") >> levels
    factors, width, hidden_local = up.shape
    tokens, columns = acts_prev.shape
    half, quarter = tokens // 2, tokens // 4
    sections = lax.axis_size("section")
    first, last = 0, sections - 1

    crossed_g = exchanged(grads_next, mask, range(1, sections))
    crossed_loss = exchanged(loss_grad, mask, range(1))
    acts_a, acts_b = join([[(0, 0, half)], [(0, half, tokens - half)]], (acts_prev,), ())
    came_a = shifted(acts_a, 1)
    came_b = shifted(acts_b, 1)
    came_g = shifted(grads_next, -1)
    up, embedded = load((up, embedded), (acts_a,))
    own_a = pick(first, (embedded, 0), (came_a, 0), half)
    their_a = swapped(own_a, mask)
    down, loss_grad = load((down, loss_grad), (own_a,))
    own_b = pick(first, (embedded, half), (came_b, 0), tokens - half, (down,))
    their_b = swapped(own_b, mask)
    onward_g = lax.ppermute(
        pick(first, (crossed_loss, 0), (crossed_g, 0), tokens, (own_b,)),
        "section",
        [(s, (s - 1) % sections) for s in range(sections)],
    )
    own_g = pick(last, (loss_grad, 0), (came_g, 0), tokens, (own_b,), COST_G)

    def forward(own, theirs, cost, after):
        shape = own.shape
        return in_vmem(
            forward_kernel,
            ([own], [theirs]),
            (up, down),
            [jax.ShapeDtypeStruct(shape, F32), jax.ShapeDtypeStruct(shape, BF16)],
            cost,
            after,
        )

    base_a, sent_a = forward(own_a, their_a, COST_A, (own_b, own_g))
    arrived_a = swapped(sent_a, mask)
    base_b, sent_b = forward(own_b, their_b, COST_B, (sent_a,))
    arrived_b = swapped(sent_b, mask)
    rows = ([own_a, own_b], [their_a, their_b], [own_g], [onward_g])
    base_back, sent_back, hidden, grad_pre = in_vmem(
        backward_kernel,
        rows,
        (up, down),
        [
            jax.ShapeDtypeStruct((tokens, columns), F32),
            jax.ShapeDtypeStruct((tokens, columns), BF16),
            jax.ShapeDtypeStruct((tokens, hidden_local), BF16),
            jax.ShapeDtypeStruct((tokens, hidden_local), BF16),
        ],
        COST_BACK,
        (sent_b,),
    )
    arrived_back = [
        swapped(sent_back[i * quarter : (i + 1) * quarter], mask) for i in range(4)
    ]
    up_grad, down_grad = run(
        weight_kernel,
        rows,
        (hidden, grad_pre),
        [jax.ShapeDtypeStruct(w.shape, BF16) for w in (up, down)],
        width,
        0,
    )
    mixed = finish(base_a, [arrived_a], 0, tokens, None, (up_grad,))
    mixed = finish(base_b, [arrived_b], half, tokens, mixed)
    end = 3 * quarter
    input_grads = finish(base_back[:end], arrived_back[:3], 0, tokens, None, (mixed,))
    input_grads = finish(base_back[end:], arrived_back[3:], end, tokens, input_grads)
    return (mixed, input_grads, up_grad[None], down_grad[None])


def solution(mesh):
    in_specs = (
        P("section", "tensor"),
        P(None, "tensor"),
        P("section", "tensor"),
        P(None, "tensor"),
        P("section", None, None, "tensor"),
        P("section", None, "tensor", None),
    )
    out_specs = (
        P("section", "tensor"),
        P("section", "tensor"),
        P("section", None, None, "tensor"),
        P("section", None, "tensor", None),
    )
    return jax.shard_map(
        on_device, mesh=mesh, in_specs=in_specs, out_specs=out_specs, check_vma=False
    )
```

```python
import math

import jax
import jax.numpy as jnp
from jax import lax
from jax.experimental import pallas as pl
from jax.experimental.pallas import tpu as pltpu
from jax.sharding import PartitionSpec as P

COST_A = 3 * 10**9
COST_G = 10**9
COST_B = 7 * 10**9
COST_BACK = 6 * 10**9
LIMIT = 8
BYTES = 8 * 2**20
TANH_SCALE = math.sqrt(2.0 / math.pi)
CUBIC = 0.044715
F32 = jnp.float32
BF16 = jnp.bfloat16


def shifted(value, by):
    length = lax.axis_size("section")
    pairs = [(i, i + by) for i in range(length) if 0 <= i + by < length]
    return lax.ppermute(value, "section", pairs)


def swapped(value, mask):
    pairs = [(source, source ^ mask) for source in range(lax.axis_size("tensor"))]
    return lax.ppermute(value, "tensor", pairs)


def exchanged(value, mask, sections, otherwise):
    size = lax.axis_size("tensor")
    pairs = []
    for s in range(lax.axis_size("section")):
        distance = mask if s in sections else otherwise
        pairs += [(s * size + t, s * size + (t ^ distance)) for t in range(size)]
    return lax.ppermute(value, ("section", "tensor"), pairs)


def mm(a, b, contract):
    return lax.dot_general(a, b, ((contract[:1], contract[1:]), ((), ())), preferred_element_type=F32)


def rows_of(refs):
    return jnp.concatenate([ref[...] for ref in refs], axis=0)


def pick(edge, at_edge, elsewhere, rows, after=(), cost=0):
    (one, one_start), (other, other_start) = at_edge, elsewhere

    def kernel(a, b, *rest):
        there = lax.axis_index("section") == edge
        rest[-1][...] = jnp.where(
            there, a[one_start : one_start + rows, :], b[other_start : other_start + rows, :]
        )

    vmem = pl.BlockSpec(memory_space=pltpu.VMEM)
    return pl.pallas_call(
        kernel,
        in_specs=[vmem, vmem] + [pl.BlockSpec(memory_space=pl.ANY)] * len(after),
        out_specs=vmem,
        out_shape=jax.ShapeDtypeStruct((rows, one.shape[1]), one.dtype),
        compiler_params=pltpu.CompilerParams(vmem_limit_bytes=8 * 2**20),
        cost_estimate=pl.CostEstimate(flops=cost, bytes_accessed=0, transcendentals=0),
    )(one, other, *after)


def join(outs_wanted, args, after, cost=0):
    columns = args[0].shape[1]

    def kernel(*refs):
        for wanted, out in zip(outs_wanted, refs[len(args) + len(after) :]):
            at = 0
            for arg, start, rows in wanted:
                out[at : at + rows, :] = refs[arg][start : start + rows, :]
                at += rows

    vmem = pl.BlockSpec(memory_space=pltpu.VMEM)
    return pl.pallas_call(
        kernel,
        in_specs=[vmem] * len(args) + [pl.BlockSpec(memory_space=pl.ANY)] * len(after),
        out_specs=[vmem] * len(outs_wanted),
        out_shape=[
            jax.ShapeDtypeStruct((sum(w[2] for w in wanted), columns), args[0].dtype)
            for wanted in outs_wanted
        ],
        compiler_params=pltpu.CompilerParams(vmem_limit_bytes=8 * 2**20),
        cost_estimate=pl.CostEstimate(flops=cost, bytes_accessed=BYTES, transcendentals=0),
    )(*args, *after)


def gate(v):
    return jnp.tanh(TANH_SCALE * (v + CUBIC * (v * v * v)))


def split(refs, counts):
    groups = []
    for count in counts:
        groups.append(refs[:count])
        refs = refs[count:]
    return groups + [refs]


def columns_of(refs, block):
    return jnp.concatenate([ref[:, block] for ref in refs], axis=0)


def over_blocks(width, columns, expand, body):
    @pl.loop(0, columns // width)
    def _(m):
        model = pl.ds(pl.multiple_of(m * width, width), width)
        body(
            model,
            [pl.ds(pl.multiple_of((m * expand + e) * width, width), width) for e in range(expand)],
        )


def forward_kernel(counts, *refs):
    own, theirs, rest = split(refs, counts)
    up, down = rest[:2]
    base, sent = rest[-2:]
    width, columns = up.shape[1], base.shape[1]

    def body(model, blocks):
        x = jnp.concatenate([columns_of(own, model), columns_of(theirs, model)], axis=1)
        kept = x[:, :width].astype(F32)
        away = jnp.zeros((x.shape[0], width), F32)
        for block in blocks:
            pre = mm(x, up[:, :, block].reshape(2 * width, width), (1, 0))
            hidden = (0.5 * pre * (1.0 + gate(pre))).astype(BF16)
            kept = kept + mm(hidden, down[0, block, :], (1, 0))
            away = away + mm(hidden, down[1, block, :], (1, 0))
        base[:, model] = kept
        sent[:, model] = away.astype(BF16)

    over_blocks(width, columns, up.shape[2] // columns, body)


def backward_kernel(counts, *refs):
    own_x, their_x, own_g, their_g, rest = split(refs, counts)
    up, down = rest[:2]
    base, sent, hidden_out, grad_pre_out = rest[-4:]
    width, columns = up.shape[1], base.shape[1]

    def body(model, blocks):
        x = jnp.concatenate([columns_of(own_x, model), columns_of(their_x, model)], axis=1)
        own, theirs = columns_of(own_g, model), columns_of(their_g, model)
        kept = own.astype(F32)
        away = jnp.zeros((x.shape[0], width), F32)
        for block in blocks:
            pre = mm(x, up[:, :, block].reshape(2 * width, width), (1, 0))
            grad_hidden = mm(own, down[0, block, :], (1, 1)) + mm(theirs, down[1, block, :], (1, 1))
            t = gate(pre)
            half = 0.5 * (1.0 + t)
            slope = half + 0.5 * pre * (1.0 - t * t) * (
                TANH_SCALE * (1.0 + 3.0 * CUBIC * (pre * pre))
            )
            grad_pre = (grad_hidden * slope).astype(BF16)
            kept = kept + mm(grad_pre, up[0, :, block], (1, 1))
            away = away + mm(grad_pre, up[1, :, block], (1, 1))
            hidden_out[:, block] = (pre * half).astype(BF16)
            grad_pre_out[:, block] = grad_pre
        base[:, model] = kept
        sent[:, model] = away.astype(BF16)

    over_blocks(width, columns, up.shape[2] // columns, body)


def in_vmem(kernel, rows, others, outs, cost, after=()):
    flat = [a for group in rows for a in group]
    vmem = pl.BlockSpec(memory_space=pltpu.VMEM)
    return pl.pallas_call(
        lambda *refs: kernel([len(group) for group in rows], *refs),
        in_specs=[vmem] * (len(flat) + len(others))
        + [pl.BlockSpec(memory_space=pl.ANY)] * len(after),
        out_specs=[vmem] * len(outs),
        out_shape=outs,
        compiler_params=pltpu.CompilerParams(vmem_limit_bytes=LIMIT * 2**20),
        cost_estimate=pl.CostEstimate(flops=cost, bytes_accessed=0, transcendentals=0),
    )(*flat, *others, *after)


def load(args, after=()):
    def kernel(*refs):
        sems = refs[-1]
        copies = [
            pltpu.make_async_copy(refs[i], refs[len(args) + len(after) + i], sems.at[i])
            for i in range(len(args))
        ]
        for copy in copies:
            copy.start()
        for copy in copies:
            copy.wait()

    return pl.pallas_call(
        kernel,
        in_specs=[pl.BlockSpec(memory_space=pl.ANY)] * (len(args) + len(after)),
        out_specs=[pl.BlockSpec(memory_space=pltpu.VMEM)] * len(args),
        out_shape=[jax.ShapeDtypeStruct(a.shape, a.dtype) for a in args],
        scratch_shapes=[pltpu.SemaphoreType.DMA((len(args),))],
        compiler_params=pltpu.CompilerParams(vmem_limit_bytes=2 * 2**20),
        cost_estimate=pl.CostEstimate(flops=0, bytes_accessed=0, transcendentals=0),
    )(*args, *after)


def weight_kernel(counts, expand, *refs):
    own_x, their_x, own_g, their_g, rest = split(refs, counts)
    hidden, grad_pre = rest[:2]
    up_grad, down_grad = rest[-2:]
    width = up_grad.shape[1]
    x = jnp.concatenate([rows_of(own_x), rows_of(their_x)], axis=1)
    g = jnp.concatenate([rows_of(own_g), rows_of(their_g)], axis=1)
    for e in range(expand):
        block = slice(e * width, (e + 1) * width)
        down_step = mm(hidden[:, block], g, (0, 0)).astype(BF16)
        down_grad[0, block, :] = down_step[:, :width]
        down_grad[1, block, :] = down_step[:, width:]
        up_step = mm(x, grad_pre[:, block], (0, 0)).astype(BF16)
        up_grad[0, :, block] = up_step[:width]
        up_grad[1, :, block] = up_step[width:]


def run(kernel, rows, others, outs, width, cost, after=()):
    flat = [a for group in rows for a in group]
    model_local = flat[0].shape[1] // width

    def spec(a):
        if len(a.shape) == 2:
            return pl.BlockSpec((a.shape[0], a.shape[1] // model_local), lambda m: (0, m))
        if a.shape[2] == width:
            return pl.BlockSpec((a.shape[0], a.shape[1] // model_local, width), lambda m: (0, m, 0))
        return pl.BlockSpec((a.shape[0], width, a.shape[2] // model_local), lambda m: (0, 0, m))

    expand = max(max(a.shape) for a in others) // (width * model_local)
    return pl.pallas_call(
        lambda *refs: kernel([len(group) for group in rows], expand, *refs),
        grid=(model_local,),
        in_specs=[spec(a) for a in (*flat, *others)]
        + [pl.BlockSpec(memory_space=pl.ANY)] * len(after),
        out_specs=[spec(a) for a in outs],
        out_shape=outs,
        compiler_params=pltpu.CompilerParams(vmem_limit_bytes=20 * 2**20),
        cost_estimate=pl.CostEstimate(flops=cost, bytes_accessed=BYTES, transcendentals=0),
    )(*flat, *others, *after)


def finish(base, pieces, start, total, result=None, after=()):
    rows, columns = base.shape

    def kernel(*refs):
        base_ref, piece_refs = refs[0], refs[1 : 1 + len(pieces)]
        out, rounded, sem = refs[-3:]
        rounded[...] = (base_ref[...] + rows_of(piece_refs).astype(F32)).astype(BF16)
        copy = pltpu.make_async_copy(rounded, out.at[pl.ds(start, rows)], sem)
        copy.start()
        copy.wait()

    vmem, anywhere = pl.BlockSpec(memory_space=pltpu.VMEM), pl.BlockSpec(memory_space=pl.ANY)
    rest = after if result is None else (result, *after)
    return pl.pallas_call(
        kernel,
        in_specs=[vmem] * (1 + len(pieces)) + [anywhere] * len(rest),
        out_specs=anywhere,
        out_shape=jax.ShapeDtypeStruct((total, columns), BF16),
        scratch_shapes=[pltpu.VMEM((rows, columns), BF16), pltpu.SemaphoreType.DMA],
        input_output_aliases={} if result is None else {1 + len(pieces): 0},
        compiler_params=pltpu.CompilerParams(vmem_limit_bytes=8 * 2**20),
        cost_estimate=pl.CostEstimate(flops=0, bytes_accessed=0, transcendentals=0),
    )(base, *pieces, *rest)


def on_device(acts_prev, embedded, grads_next, loss_grad, up_weight, down_weight):
    up, down = up_weight[0], down_weight[0]
    levels = up.shape[0] - 1
    mask = lax.axis_size("tensor") >> levels
    factors, width, hidden_local = up.shape
    tokens, columns = acts_prev.shape
    half = tokens // 2
    sections = lax.axis_size("section")
    first, last = 0, sections - 1

    crossed_g = exchanged(grads_next, mask, range(1, sections), 2)
    crossed_loss = exchanged(loss_grad, mask, range(1), 1)
    acts_a, acts_b = join([[(0, 0, half)], [(0, half, tokens - half)]], (acts_prev,), ())
    came_a = shifted(acts_a, 1)
    came_b = shifted(acts_b, 1)
    came_g = shifted(grads_next, -1)
    up, embedded = load((up, embedded), (acts_a,))
    own_a = pick(first, (embedded, 0), (came_a, 0), half)
    their_a = swapped(own_a, mask)
    down, loss_grad = load((down, loss_grad), (own_a,))
    own_b = pick(first, (embedded, half), (came_b, 0), tokens - half, (down,))
    their_b = swapped(own_b, mask)
    onward_g = lax.ppermute(
        pick(first, (crossed_loss, 0), (crossed_g, 0), tokens, (own_b,)),
        "section",
        [(s, (s - 1) % sections) for s in range(sections)],
    )
    own_g = pick(last, (loss_grad, 0), (came_g, 0), tokens, (own_b,), COST_G)

    def forward(own, theirs, cost, after):
        shape = own.shape
        return in_vmem(
            forward_kernel,
            ([own], [theirs]),
            (up, down),
            [jax.ShapeDtypeStruct(shape, F32), jax.ShapeDtypeStruct(shape, BF16)],
            cost,
            after,
        )

    base_a, sent_a = forward(own_a, their_a, COST_A, (own_b, own_g))
    arrived_a = swapped(sent_a, mask)
    base_b, sent_b = forward(own_b, their_b, COST_B, (sent_a,))
    arrived_b = swapped(sent_b, mask)
    rows = ([own_a, own_b], [their_a, their_b], [own_g], [onward_g])
    base_back, sent_back, hidden, grad_pre = in_vmem(
        backward_kernel,
        rows,
        (up, down),
        [
            jax.ShapeDtypeStruct((tokens, columns), F32),
            jax.ShapeDtypeStruct((tokens, columns), BF16),
            jax.ShapeDtypeStruct((tokens, hidden_local), BF16),
            jax.ShapeDtypeStruct((tokens, hidden_local), BF16),
        ],
        COST_BACK,
        (sent_b,),
    )
    ends = [tokens * i // 32 for i in (11, 22, 30, 32)]
    arrived_back = [
        swapped(sent_back[at:end], mask) for at, end in zip([0] + ends[:-1], ends)
    ]
    up_grad, down_grad = run(
        weight_kernel,
        rows,
        (hidden, grad_pre),
        [jax.ShapeDtypeStruct(w.shape, BF16) for w in (up, down)],
        width,
        0,
    )
    mixed = finish(base_a, [arrived_a], 0, tokens, None, (up_grad,))
    mixed = finish(base_b, [arrived_b], half, tokens, mixed)
    input_grads = finish(base_back[: ends[1]], arrived_back[:2], 0, tokens, None, (mixed,))
    for i in range(2, len(ends)):
        start, end = ends[i - 1], ends[i]
        input_grads = finish(base_back[start:end], arrived_back[i : i + 1], start, tokens, input_grads)
    return (mixed, input_grads, up_grad[None], down_grad[None])


def solution(mesh):
    in_specs = (
        P("section", "tensor"),
        P(None, "tensor"),
        P("section", "tensor"),
        P(None, "tensor"),
        P("section", None, None, "tensor"),
        P("section", None, "tensor", None),
    )
    out_specs = (
        P("section", "tensor"),
        P("section", "tensor"),
        P("section", None, None, "tensor"),
        P("section", None, "tensor", None),
    )
    return jax.shard_map(
        on_device, mesh=mesh, in_specs=in_specs, out_specs=out_specs, check_vma=False
    )
```
